32 devices in a mesh: pipe: 4 (over y, core), node: 4 (over z), ep: 2 (over x).
Axes of the slice: x: 2, y: 2, z: 4, core: 2. Of those that a mesh axis runs over, the one named last changes fastest.
Arguments:
- grad_tokens: bfloat16 [4, 4, 2, 128, 7168], P('pipe', 'node', 'ep'), may hold values from -6 to 6
- slot_token: int32 [4, 4, 2, 4, 8], P('pipe', 'node', 'ep'), may hold values from 0 to 127, as said below
- send_count: int32 [4, 4, 2, 4], P('pipe', 'node', 'ep'), may hold values from 1 to 8, as said below
- route_score: float32 [4, 4, 2, 4, 8], P('pipe', 'node', 'ep'), may hold values from 0.05 to 1
- hidden_act: bfloat16 [4, 4, 64, 1024], P('pipe', 'node', 'ep'), may hold values from -2.390625 to 2.390625
- w_down: bfloat16 [4, 4, 1024, 7168], P('pipe', 'node', None, 'ep'), as said below
Outputs:
- grad_hidden: bfloat16 [4, 4, 64, 1024], P('pipe', 'node', 'ep')
- grad_weight: bfloat16 [4, 4, 512, 7168], P('pipe', 'node', None, 'ep')
The draws below stay inside these ranges and needn't reach their ends.
Inputs may be any that keep to these rules, and one draw needn't show every extreme that they name: `slot_token`: the 8 entries for one device and one node group are distinct tokens of that device; only the first send_count of them are sent. `send_count`: in every section one node group, drawn from the seed, receives 8 rows from every device of the section; every other count is at most 5. w_down[p] equals w_down[3 - p].
All inputs are finite; a program needn't handle non-finite values.
Results may differ from the reference program's by a relative error of at most 0.0059.
Values may be sent and summed in bfloat16 or wider, within the bound.
A program may use at most 128 MiB of HBM per device.

```python
import jax
import jax.numpy as jnp
from jax import lax

D = 7168
FE = 1024
TOK_DEV = 128
CAP = 8
RECV = 64
N_PIPE = 4
N_NODE = 4
N_EP = 2


def draw_slot_token(key, part):
    key = jax.random.fold_in(key, 11)
    number = N_PIPE * N_NODE * N_EP * N_NODE
    keys = jax.random.split(key, number)
    picked = jax.vmap(lambda one_key: jax.random.permutation(one_key, TOK_DEV)[:CAP])(keys)
    return picked.reshape(N_PIPE, N_NODE, N_EP, N_NODE, CAP).astype(jnp.int32)


def draw_send_count(key, part):
    key = jax.random.fold_in(key, 12)
    hot_key, count_key = jax.random.split(key)
    hot_group = jax.random.randint(hot_key, (N_PIPE,), 0, N_NODE)
    counts = jax.random.randint(count_key, (N_PIPE, N_NODE, N_EP, N_NODE), 1, max(2 * CAP // 3, 1) + 1)
    is_hot = jnp.arange(N_NODE)[None, :] == hot_group[:, None]
    return jnp.where(is_hot[:, None, None, :], CAP, counts).astype(jnp.int32)


def draw_w_down(key, part):
    key = jax.random.fold_in(key, 13)
    shape_half = (N_PIPE // 2, N_NODE, FE, D)
    factor = FE ** (-0.5)
    base = jax.random.normal(key, shape_half, jnp.float32) * factor
    base = base.astype(jnp.bfloat16)
    return jnp.concatenate([base, base[::-1]], axis=0)


def level_of(stream_key, extent, cuts, low, top_value):
    def one(axis_at, shards_of):
        draws = jax.random.uniform(jax.random.fold_in(jax.random.fold_in(stream_key, 6), axis_at), (shards_of,), jnp.float32, low / len(cuts), top_value / len(cuts))
        return jnp.repeat(jnp.exp(draws), extent[axis_at] // shards_of).reshape((-1,) + (1,) * (len(extent) - axis_at - 1))

    level = one(*cuts[0])
    for cut in cuts[1:]:
        level = level * one(*cut)
    return level


def centred(rng, shape, width, bound, shards=(), kind=jnp.bfloat16):
    entries = width * jax.random.normal(rng, shape, jnp.float32)
    if shards:
        entries = entries * level_of(rng, shape, shards, -0.22, 0.18)
    return jnp.clip(entries, -bound, bound).astype(kind)


def setup_inputs(seed: int = 0) -> dict:
    splits = jax.random.split(jax.random.key(seed), 7)
    grad_tokens = centred(splits[0], (N_PIPE, N_NODE, N_EP, TOK_DEV, D), 1.0, 6.0, ((0, 4), (1, 4), (2, 2)))
    slot_token = draw_slot_token(jax.random.fold_in(splits[6], 71), 0)
    send_count = draw_send_count(jax.random.fold_in(splits[6], 71), 0)
    route_score = jnp.clip(0.05 + 0.95 * jax.random.uniform(splits[3], (N_PIPE, N_NODE, N_EP, N_NODE, CAP), jnp.float32) ** level_of(splits[3], (N_PIPE, N_NODE, N_EP, N_NODE, CAP), ((0, 4), (1, 4), (2, 2)), -0.2, 0.2), 0.05, 1.0)
    hidden_act = centred(splits[4], (N_PIPE, N_NODE, RECV, FE), 0.3, 2.390625, ((0, 4), (1, 4), (2, 2)))
    w_down = draw_w_down(jax.random.fold_in(splits[6], 71), 0)
    return {"grad_tokens": grad_tokens, "slot_token": slot_token, "send_count": send_count, "route_score": route_score, "hidden_act": hidden_act, "w_down": w_down}


def route_rows(tokens_section, slots_section, counts_section, scores_section, group):
    slots_dest = lax.dynamic_index_in_dim(slots_section, group, 2, False)
    counts_dest = lax.dynamic_index_in_dim(counts_section, group, 2, False)
    scores_dest = lax.dynamic_index_in_dim(scores_section, group, 2, False)
    picked = jnp.take_along_axis(tokens_section, slots_dest[..., None].astype(jnp.int32), axis=2)
    live_slots = jnp.arange(CAP, dtype=jnp.int32)[None, None, :] < counts_dest[..., None]
    factor = jnp.where(live_slots, scores_dest, jnp.zeros_like(scores_dest))
    routed = (picked.astype(jnp.float32) * factor[..., None].astype(jnp.float32)).astype(jnp.bfloat16)
    return routed.reshape(RECV, D)


def reference(grad_tokens, slot_token, send_count, route_score, hidden_act, w_down):
    def section_work(section_args):
        tokens_section, slots_section, counts_section, scores_section, hidden_section, weight_section = section_args

        def group_work(inner):
            group, hidden_group, weight_group = inner
            routed = route_rows(tokens_section, slots_section, counts_section, scores_section, group)
            grad_h = jnp.dot(routed, weight_group.T, preferred_element_type=jnp.float32).astype(jnp.bfloat16)
            weight_part = jnp.dot(hidden_group.T, routed, preferred_element_type=jnp.float32).astype(jnp.bfloat16)
            return grad_h, weight_part

        return lax.map(group_work, (jnp.arange(N_NODE, dtype=jnp.int32), hidden_section, weight_section))

    grad_hidden, parts = lax.map(section_work, (grad_tokens, slot_token, send_count, route_score, hidden_act, w_down))
    half_rows = FE // 2
    middle = N_PIPE // 2
    lower_sum = parts[:middle, :, :half_rows].astype(jnp.float32) + parts[middle:][::-1][:, :, :half_rows].astype(jnp.float32)
    upper_sum = parts[middle:, :, half_rows:].astype(jnp.float32) + parts[:middle][::-1][:, :, half_rows:].astype(jnp.float32)
    grad_weight = jnp.concatenate([lower_sum, upper_sum], axis=0).astype(jnp.bfloat16)
    return grad_hidden, grad_weight
```

```python
import functools

import jax
import jax.numpy as jnp
from jax import lax
from jax.experimental import pallas as pl
from jax.experimental.pallas import tpu as pltpu
from jax.sharding import PartitionSpec as P

MESH = pl.DeviceIdType.MESH
AXES = ("pipe", "node", "ep")


def flip(index, mask):
    out = index
    bit = 1
    while bit <= mask:
        if mask & bit:
            out = out + bit * (1 - 2 * ((index // bit) % 2))
        bit *= 2
    return out


def relay_kernel(
    sizes,
    parts,
    tokens,
    slots,
    counts,
    scores,
    hidden,
    weight,
    grad_hidden,
    rows_out,
    hidden_out,
    tok_v,
    weight_v,
    send,
    recv,
    mirrored,
    hid,
    total,
    part_send,
    part_recv,
    tok_sem,
    weight_sem,
    send_sem,
    recv_sem,
    fwd_sem,
    mir_sem,
    hsend_sem,
    hrecv_sem,
    hloc_sem,
    psend_sem,
    precv_sem,
):
    n_pipe, n_node, n_ep = sizes
    n_src = n_node * n_ep
    cap, piece = send.shape[2], send.shape[3]
    width = piece * parts
    tok_rows = tok_v.shape[0]
    own_rows = hid.shape[2]
    half = hid.shape[3]
    recv_rows = n_src * cap

    pipe, node, ep = (lax.axis_index(name) for name in AXES)
    mirror = n_pipe - 1 - pipe
    me = node * n_ep + ep
    keep_first = (pipe // (n_pipe // 2)) * half
    give_first = half - keep_first

    tok_loads = {}
    for c in range(parts):
        for e in range(n_ep):
            cols = pl.ds(e * width + c * piece, piece)
            tok_loads[c, e] = pltpu.make_async_copy(
                tokens.at[0, 0, 0, :, cols], tok_v.at[:, cols], tok_sem.at[c, e]
            )
            tok_loads[c, e].start()
    hid_load = pltpu.make_async_copy(
        hidden.at[0, 0, :, pl.ds(pl.multiple_of(keep_first, 128), half)],
        hid.at[0, ep],
        hloc_sem,
    )
    hid_load.start()
    weight_loads = []
    for c in range(parts):
        cols = pl.ds(c * piece, piece)
        load = pltpu.make_async_copy(
            weight.at[0, 0, :, cols], weight_v.at[:, cols], weight_sem.at[c]
        )
        load.start()
        weight_loads.append(load)

    barrier = pltpu.get_barrier_semaphore()
    peers = [
        (pipe, flip(node, k), flip(ep, j))
        for k in range(n_node)
        for j in range(n_ep)
        if k or j
    ] + [(mirror, node, flip(ep, j)) for j in range(n_ep)]
    for peer in peers:
        pl.semaphore_signal(barrier, inc=1, device_id=peer, device_id_type=MESH)

    eye = lax.broadcasted_iota(jnp.int32, (cap, cap), 0) == lax.broadcasted_iota(
        jnp.int32, (cap, cap), 1
    )
    slot_ids = lax.broadcasted_iota(jnp.int32, (cap, 1), 0)
    token_ids = lax.broadcasted_iota(jnp.int32, (cap, tok_rows), 1)
    hot, factor = [], []
    for g in range(n_node):
        slot_row = slots[0, 0, 0, g : g + 1, :]
        score_row = scores[0, 0, 0, g : g + 1, :]
        slot_col = jnp.sum(jnp.where(eye, slot_row, 0), axis=1, keepdims=True)
        score_col = jnp.sum(jnp.where(eye, score_row, 0.0), axis=1, keepdims=True)
        hot.append(jnp.where(token_ids == slot_col, 1.0, 0.0))
        factor.append(jnp.where(slot_ids < counts[0, 0, 0, g], score_col, 0.0))
    hot = jnp.concatenate(hot, axis=0).astype(jnp.bfloat16)
    factor = jnp.concatenate(factor, axis=0)

    def route(c):
        for e in range(n_ep):
            tok_loads[c, e].wait()
            start = e * width + c * piece
            picked = jnp.dot(
                hot, tok_v[:, start : start + piece], preferred_element_type=jnp.float32
            )
            picked = picked * factor
            for g in range(n_node):
                send[c, g * n_ep + e] = picked[g * cap : (g + 1) * cap].astype(jnp.bfloat16)

    sent = []

    def dispatch(c):
        for k in reversed(range(n_node)):
            for j in reversed(range(n_ep)):
                if k == 0 and j == 0:
                    continue
                to_node, to_ep = flip(node, k), flip(ep, j)
                copy = pltpu.make_async_remote_copy(
                    src_ref=send.at[c, to_node * n_ep + to_ep],
                    dst_ref=recv.at[c, me],
                    send_sem=send_sem.at[c, k * n_ep + j],
                    recv_sem=recv_sem.at[c, me],
                    device_id=(pipe, to_node, to_ep),
                    device_id_type=MESH,
                )
                copy.start()
                sent.append(copy)

    def forward(c, source, index, block):
        copy = pltpu.make_async_remote_copy(
            src_ref=block,
            dst_ref=mirrored.at[c, source],
            send_sem=fwd_sem.at[c, index],
            recv_sem=mir_sem.at[c, source],
            device_id=(mirror, node, ep),
            device_id_type=MESH,
        )
        copy.start()
        sent.append(copy)

    route(0)
    pl.semaphore_wait(barrier, len(peers))
    dispatch(0)
    forward(0, me, 0, send.at[0, me])
    for j in range(n_ep):
        copy = pltpu.make_async_remote_copy(
            src_ref=hidden.at[0, 0, :, pl.ds(pl.multiple_of(give_first, 128), half)],
            dst_ref=hid.at[1, ep],
            send_sem=hsend_sem.at[1, j],
            recv_sem=hrecv_sem.at[1, ep],
            device_id=(mirror, node, flip(ep, j)),
            device_id_type=MESH,
        )
        copy.start()
        sent.append(copy)
        if j:
            copy = pltpu.make_async_remote_copy(
                src_ref=hidden.at[0, 0, :, pl.ds(pl.multiple_of(keep_first, 128), half)],
                dst_ref=hid.at[0, ep],
                send_sem=hsend_sem.at[0, j],
                recv_sem=hrecv_sem.at[0, ep],
                device_id=(pipe, node, flip(ep, j)),
                device_id_type=MESH,
            )
            copy.start()
            sent.append(copy)
    for c in range(1, parts):
        route(c)
        dispatch(c)
        forward(c, me, 0, send.at[c, me])
    for c in range(parts):
        recv[c, me] = send[c, me]

    def arrival(buffer, index, sem):
        return pltpu.make_async_remote_copy(
            src_ref=buffer.at[index],
            dst_ref=buffer.at[index],
            send_sem=send_sem.at[0, 0],
            recv_sem=sem.at[index],
            device_id=(mirror, node, ep),
            device_id_type=MESH,
        )

    def gathered(buffer, c):
        blocks = [buffer[c, s].astype(jnp.float32) for s in range(n_src)]
        return jnp.concatenate(blocks, axis=0).astype(jnp.bfloat16)

    for c in range(parts):
        for k in range(n_node):
            for j in range(n_ep):
                if k == 0 and j == 0:
                    continue
                source = flip(node, k) * n_ep + flip(ep, j)
                arrival(recv, (c, source), recv_sem).wait_recv()
                forward(c, source, k * n_ep + j, recv.at[c, source])
        rows = gathered(recv, c)
        rows_out[0:recv_rows, c * piece : (c + 1) * piece] = rows
        weight_loads[c].wait()
        share = lax.dot_general(
            rows,
            weight_v[:, c * piece : (c + 1) * piece],
            (((1,), (1,)), ((), ())),
            preferred_element_type=jnp.float32,
        )
        if c == 0:
            total[...] = share
        else:
            total[...] += share

    for j in range(1, n_ep):
        to_ep = flip(ep, j)
        first = pl.multiple_of(to_ep * own_rows, own_rows)
        part_send[j] = total[pl.ds(first, own_rows), :].astype(jnp.bfloat16)
        copy = pltpu.make_async_remote_copy(
            src_ref=part_send.at[j],
            dst_ref=part_recv.at[ep],
            send_sem=psend_sem.at[j],
            recv_sem=precv_sem.at[ep],
            device_id=(pipe, node, to_ep),
            device_id_type=MESH,
        )
        copy.start()
        sent.append(copy)

    hid_load.wait()
    for j in range(n_ep):
        source = flip(ep, j)
        arrival(hid, (1, source), hrecv_sem).wait_recv()
        if j:
            arrival(hid, (0, source), hrecv_sem).wait_recv()
    for copy_at in range(2):
        for e in range(n_ep):
            first = (copy_at * n_ep + e) * own_rows
            hidden_out[first : first + own_rows, :] = hid[copy_at, e]

    for c in range(parts):
        for k in range(n_node):
            for j in range(n_ep):
                source = flip(node, k) * n_ep + flip(ep, j)
                arrival(mirrored, (c, source), mir_sem).wait_recv()
        rows_out[recv_rows:, c * piece : (c + 1) * piece] = gathered(mirrored, c)

    first = pl.multiple_of(ep * own_rows, own_rows)
    own = total[pl.ds(first, own_rows), :]
    for j in range(1, n_ep):
        source = flip(ep, j)
        arrival(part_recv, (source,), precv_sem).wait_recv()
        own = own + part_recv[source].astype(jnp.float32)
    grad_hidden[0, 0] = own.astype(jnp.bfloat16)
    for copy in sent:
        copy.wait_send()


def weight_kernel(hidden, rows, out):
    out[0, 0] = lax.dot_general(
        hidden[...], rows[...], (((0,), (0,)), ((), ())), preferred_element_type=jnp.float32
    ).astype(jnp.bfloat16)


def local(sizes, grad_tokens, slot_token, send_count, route_score, hidden_act, w_down):
    n_pipe, n_node, n_ep = sizes
    n_src = n_node * n_ep
    tok_rows, features = grad_tokens.shape[-2:]
    cap = slot_token.shape[-1]
    own_rows, units = hidden_act.shape[-2:]
    width = w_down.shape[-1]
    half = units // 2
    recv_rows = n_src * cap
    parts = 2 if (width // 128) % 2 == 0 else 1
    piece = width // parts
    bf16, f32 = jnp.bfloat16, jnp.float32
    dma = pltpu.SemaphoreType.DMA
    vmem = pl.BlockSpec(memory_space=pltpu.VMEM)
    hbm = pl.BlockSpec(memory_space=pl.ANY)
    grad_hidden, rows, hidden = pl.pallas_call(
        functools.partial(relay_kernel, sizes, parts),
        out_shape=(
            jax.ShapeDtypeStruct((1, 1, own_rows, units), bf16),
            jax.ShapeDtypeStruct((2 * recv_rows, width), bf16),
            jax.ShapeDtypeStruct((2 * recv_rows, half), bf16),
        ),
        in_specs=[hbm, vmem, pl.BlockSpec(memory_space=pltpu.SMEM), vmem, hbm, hbm],
        out_specs=(vmem, vmem, vmem),
        scratch_shapes=[
            pltpu.VMEM((tok_rows, features), bf16),
            pltpu.VMEM((units, width), bf16),
            pltpu.VMEM((parts, n_src, cap, piece), bf16),
            pltpu.VMEM((parts, n_src, cap, piece), bf16),
            pltpu.VMEM((parts, n_src, cap, piece), bf16),
            pltpu.VMEM((2, n_ep, own_rows, half), bf16),
            pltpu.VMEM((recv_rows, units), f32),
            pltpu.VMEM((n_ep, own_rows, units), bf16),
            pltpu.VMEM((n_ep, own_rows, units), bf16),
            dma((parts, n_ep)),
            dma((parts,)),
            dma((parts, n_src)),
            dma((parts, n_src)),
            dma((parts, n_src)),
            dma((parts, n_src)),
            dma((2, n_ep)),
            dma((2, n_ep)),
            dma,
            dma((n_ep,)),
            dma((n_ep,)),
        ],
        compiler_params=pltpu.CompilerParams(
            collective_id=0, has_side_effects=True, vmem_limit_bytes=40 * 2**20
        ),
    )(grad_tokens, slot_token, send_count, route_score, hidden_act, w_down)

    tile = 512 if width % 512 == 0 else 128
    grad_weight = pl.pallas_call(
        weight_kernel,
        grid=(width // tile,),
        out_shape=jax.ShapeDtypeStruct((1, 1, half, width), bf16),
        in_specs=[
            pl.BlockSpec((2 * recv_rows, half), lambda i: (0, 0)),
            pl.BlockSpec((2 * recv_rows, tile), lambda i: (0, i)),
        ],
        out_specs=pl.BlockSpec((1, 1, half, tile), lambda i: (0, 0, 0, i)),
        compiler_params=pltpu.CompilerParams(vmem_limit_bytes=24 * 2**20),
    )(hidden, rows)
    return grad_hidden, grad_weight


def solution(mesh):
    sizes = tuple(mesh.shape[name] for name in AXES)
    in_specs = (
        P("pipe", "node", "ep", None, None),
        P("pipe", "node", "ep", None, None),
        P("pipe", "node", "ep", None),
        P("pipe", "node", "ep", None, None),
        P("pipe", "node", "ep", None),
        P("pipe", "node", None, "ep"),
    )
    out_specs = (P("pipe", "node", "ep", None), P("pipe", "node", None, "ep"))
    return jax.shard_map(
        functools.partial(local, sizes),
        mesh=mesh,
        in_specs=in_specs,
        out_specs=out_specs,
        check_vma=False,
    )
```

```python
import functools

import jax
import jax.numpy as jnp
from jax import lax
from jax.experimental import pallas as pl
from jax.experimental.pallas import tpu as pltpu
from jax.sharding import PartitionSpec as P

MESH = pl.DeviceIdType.MESH
AXES = ("pipe", "node", "ep")


def flip(index, mask):
    out = index
    bit = 1
    while bit <= mask:
        if mask & bit:
            out = out + bit * (1 - 2 * ((index // bit) % 2))
        bit *= 2
    return out


def relay_kernel(
    sizes,
    parts,
    tokens,
    slots,
    counts,
    scores,
    hidden,
    weight,
    grad_hidden,
    rows_out,
    hidden_out,
    slots_v,
    counts_v,
    scores_v,
    tok_v,
    weight_v,
    send,
    recv,
    mirrored,
    hid,
    hid_all,
    hid_turned,
    rows_all,
    total,
    part_send,
    part_recv,
    small_sem,
    tok_sem,
    weight_sem,
    send_sem,
    recv_sem,
    fwd_sem,
    mir_sem,
    hsend_sem,
    hrecv_sem,
    hloc_sem,
    rows_sem,
    turned_sem,
    psend_sem,
    precv_sem,
):
    n_pipe, n_node, n_ep = sizes
    n_src = n_node * n_ep
    cap, piece = send.shape[2], send.shape[3]
    width = piece * parts
    tok_rows = tok_v.shape[0]
    own_rows = hid.shape[2]
    half = hid.shape[3]
    recv_rows = n_src * cap

    pipe, node, ep = (lax.axis_index(name) for name in AXES)
    mirror = n_pipe - 1 - pipe
    me = node * n_ep + ep
    keep_first = (pipe // (n_pipe // 2)) * half
    give_first = half - keep_first

    small_loads = [
        pltpu.make_async_copy(slots.at[0, 0, 0], slots_v, small_sem.at[0]),
        pltpu.make_async_copy(counts.at[0, 0], counts_v, small_sem.at[1]),
        pltpu.make_async_copy(scores.at[0, 0, 0], scores_v, small_sem.at[2]),
    ]
    for load in small_loads:
        load.start()
    tok_loads = {}
    for c in range(parts):
        for e in range(n_ep):
            cols = pl.ds(e * width + c * piece, piece)
            tok_loads[c, e] = pltpu.make_async_copy(
                tokens.at[0, 0, 0, :, cols], tok_v.at[:, cols], tok_sem.at[c, e]
            )
            tok_loads[c, e].start()
    hid_load = pltpu.make_async_copy(
        hidden.at[0, 0, :, pl.ds(pl.multiple_of(keep_first, 128), half)],
        hid.at[0, ep],
        hloc_sem,
    )
    hid_load.start()
    weight_loads = []
    for c in range(parts):
        cols = pl.ds(c * piece, piece)
        load = pltpu.make_async_copy(
            weight.at[0, 0, :, cols], weight_v.at[:, cols], weight_sem.at[c]
        )
        load.start()
        weight_loads.append(load)

    barrier = pltpu.get_barrier_semaphore()
    peers = [
        (pipe, flip(node, k), flip(ep, j))
        for k in range(n_node)
        for j in range(n_ep)
        if k or j
    ] + [(mirror, node, flip(ep, j)) for j in range(n_ep)]
    for peer in peers:
        pl.semaphore_signal(barrier, inc=1, device_id=peer, device_id_type=MESH)

    eye = lax.broadcasted_iota(jnp.int32, (cap, cap), 0) == lax.broadcasted_iota(
        jnp.int32, (cap, cap), 1
    )
    slot_ids = lax.broadcasted_iota(jnp.int32, (cap, 1), 0)
    token_ids = lax.broadcasted_iota(jnp.int32, (cap, tok_rows), 1)
    hot, factor = [], []
    for load in small_loads:
        load.wait()
    for g in range(n_node):
        slot_row = slots_v[g : g + 1, :]
        score_row = scores_v[g : g + 1, :]
        slot_col = jnp.sum(jnp.where(eye, slot_row, 0), axis=1, keepdims=True)
        score_col = jnp.sum(jnp.where(eye, score_row, 0.0), axis=1, keepdims=True)
        hot.append(jnp.where(token_ids == slot_col, 1.0, 0.0))
        factor.append(jnp.where(slot_ids < counts_v[0, g], score_col, 0.0))
    hot = jnp.concatenate(hot, axis=0).astype(jnp.bfloat16)
    factor = jnp.concatenate(factor, axis=0)

    def route(c):
        for e in range(n_ep):
            tok_loads[c, e].wait()
            start = e * width + c * piece
            picked = jnp.dot(
                hot, tok_v[:, start : start + piece], preferred_element_type=jnp.float32
            )
            picked = picked * factor
            for g in range(n_node):
                send[c, g * n_ep + e] = picked[g * cap : (g + 1) * cap].astype(jnp.bfloat16)

    sent, stores = [], []

    def store_rows(c, at, value):
        block = (pl.ds(at * recv_rows, recv_rows), pl.ds(c * piece, piece))
        rows_all[block] = value
        store = pltpu.make_async_copy(
            rows_all.at[block], rows_out.at[block], rows_sem.at[at, c]
        )
        store.start()
        stores.append(store)

    def dispatch(c):
        for k in range(n_node):
            for j in reversed(range(n_ep)):
                if k == 0 and j == 0:
                    continue
                to_node, to_ep = flip(node, k), flip(ep, j)
                copy = pltpu.make_async_remote_copy(
                    src_ref=send.at[c, to_node * n_ep + to_ep],
                    dst_ref=recv.at[c, me],
                    send_sem=send_sem.at[c, k * n_ep + j],
                    recv_sem=recv_sem.at[c, me],
                    device_id=(pipe, to_node, to_ep),
                    device_id_type=MESH,
                )
                copy.start()
                sent.append(copy)

    def forward(c, source, index, block):
        copy = pltpu.make_async_remote_copy(
            src_ref=block,
            dst_ref=mirrored.at[c, source],
            send_sem=fwd_sem.at[c, index],
            recv_sem=mir_sem.at[c, source],
            device_id=(mirror, node, ep),
            device_id_type=MESH,
        )
        copy.start()
        sent.append(copy)

    route(0)
    pl.semaphore_wait(barrier, len(peers))
    dispatch(0)
    forward(0, me, 0, send.at[0, me])
    for j in range(n_ep):
        copy = pltpu.make_async_remote_copy(
            src_ref=hidden.at[0, 0, :, pl.ds(pl.multiple_of(give_first, 128), half)],
            dst_ref=hid.at[1, ep],
            send_sem=hsend_sem.at[1, j],
            recv_sem=hrecv_sem.at[1, ep],
            device_id=(mirror, node, flip(ep, j)),
            device_id_type=MESH,
        )
        copy.start()
        sent.append(copy)
        if j:
            copy = pltpu.make_async_remote_copy(
                src_ref=hidden.at[0, 0, :, pl.ds(pl.multiple_of(keep_first, 128), half)],
                dst_ref=hid.at[0, ep],
                send_sem=hsend_sem.at[0, j],
                recv_sem=hrecv_sem.at[0, ep],
                device_id=(pipe, node, flip(ep, j)),
                device_id_type=MESH,
            )
            copy.start()
            sent.append(copy)
    for c in range(1, parts):
        route(c)
        dispatch(c)
        forward(c, me, 0, send.at[c, me])
    for c in range(parts):
        recv[c, me] = send[c, me]

    def arrival(buffer, index, sem):
        return pltpu.make_async_remote_copy(
            src_ref=buffer.at[index],
            dst_ref=buffer.at[index],
            send_sem=send_sem.at[0, 0],
            recv_sem=sem.at[index],
            device_id=(mirror, node, ep),
            device_id_type=MESH,
        )

    def gathered(buffer, c):
        blocks = [buffer[c, s].astype(jnp.float32) for s in range(n_src)]
        return jnp.concatenate(blocks, axis=0).astype(jnp.bfloat16)

    hid_load.wait()
    for j in range(n_ep):
        source = flip(ep, j)
        arrival(hid, (1, source), hrecv_sem).wait_recv()
        if j:
            arrival(hid, (0, source), hrecv_sem).wait_recv()
    for copy_at in range(2):
        for e in range(n_ep):
            first = (copy_at * n_ep + e) * own_rows
            hid_all[first : first + own_rows, :] = hid[copy_at, e].astype(jnp.float32)
    hid_turned[...] = hid_all[...].T.astype(jnp.bfloat16)
    store = pltpu.make_async_copy(hid_turned, hidden_out, turned_sem)
    store.start()
    stores.append(store)

    for c in range(parts):
        for k in range(n_node):
            for j in range(n_ep):
                if k == 0 and j == 0:
                    continue
                source = flip(node, k) * n_ep + flip(ep, j)
                arrival(recv, (c, source), recv_sem).wait_recv()
                forward(c, source, k * n_ep + j, recv.at[c, source])
        rows = gathered(recv, c)
        store_rows(c, 0, rows)
        weight_loads[c].wait()
        share = lax.dot_general(
            rows,
            weight_v[:, c * piece : (c + 1) * piece],
            (((1,), (1,)), ((), ())),
            preferred_element_type=jnp.float32,
        )
        if c == 0:
            total[...] = share
        else:
            total[...] += share

    for j in range(1, n_ep):
        to_ep = flip(ep, j)
        first = pl.multiple_of(to_ep * own_rows, own_rows)
        part_send[j] = total[pl.ds(first, own_rows), :].astype(jnp.bfloat16)
        copy = pltpu.make_async_remote_copy(
            src_ref=part_send.at[j],
            dst_ref=part_recv.at[ep],
            send_sem=psend_sem.at[j],
            recv_sem=precv_sem.at[ep],
            device_id=(pipe, node, to_ep),
            device_id_type=MESH,
        )
        copy.start()
        sent.append(copy)

    for c in range(parts):
        for k in range(n_node):
            for j in range(n_ep):
                source = flip(node, k) * n_ep + flip(ep, j)
                arrival(mirrored, (c, source), mir_sem).wait_recv()
        store_rows(c, 1, gathered(mirrored, c))

    first = pl.multiple_of(ep * own_rows, own_rows)
    own = total[pl.ds(first, own_rows), :]
    for j in range(1, n_ep):
        source = flip(ep, j)
        arrival(part_recv, (source,), precv_sem).wait_recv()
        own = own + part_recv[source].astype(jnp.float32)
    grad_hidden[0, 0] = own.astype(jnp.bfloat16)
    for copy in sent:
        copy.wait_send()
    for store in stores:
        store.wait()


def weight_kernel(hidden, rows, out, hid_v, rows_v, out_v, load_sem, store_sem):
    loads = [
        pltpu.make_async_copy(hidden, hid_v, load_sem.at[0]),
        pltpu.make_async_copy(rows, rows_v, load_sem.at[1]),
    ]
    for load in loads:
        load.start()
    for load in loads:
        load.wait()
    steps = store_sem.shape[0]
    tall = hid_v.shape[0] // steps
    stores = []
    for m in range(steps):
        block = pl.ds(m * tall, tall)
        out_v[block, :] = jnp.dot(
            hid_v[block, :], rows_v[...], preferred_element_type=jnp.float32
        ).astype(jnp.bfloat16)
        store = pltpu.make_async_copy(
            out_v.at[block, :], out.at[0, 0, block, :], store_sem.at[m]
        )
        store.start()
        stores.append(store)
    for store in stores:
        store.wait()


def local(sizes, grad_tokens, slot_token, send_count, route_score, hidden_act, w_down):
    n_pipe, n_node, n_ep = sizes
    n_src = n_node * n_ep
    tok_rows, features = grad_tokens.shape[-2:]
    cap = slot_token.shape[-1]
    own_rows, units = hidden_act.shape[-2:]
    width = w_down.shape[-1]
    half = units // 2
    recv_rows = n_src * cap
    parts = 2 if (width // 128) % 2 == 0 else 1
    piece = width // parts
    bf16, f32 = jnp.bfloat16, jnp.float32
    dma = pltpu.SemaphoreType.DMA
    vmem = pl.BlockSpec(memory_space=pltpu.VMEM)
    hbm = pl.BlockSpec(memory_space=pltpu.HBM)
    grad_hidden, rows, hidden = pl.pallas_call(
        functools.partial(relay_kernel, sizes, parts),
        out_shape=(
            jax.ShapeDtypeStruct((1, 1, own_rows, units), bf16),
            jax.ShapeDtypeStruct((2 * recv_rows, width), bf16),
            jax.ShapeDtypeStruct((half, 2 * recv_rows), bf16),
        ),
        in_specs=[hbm] * 6,
        out_specs=(vmem, hbm, hbm),
        scratch_shapes=[
            pltpu.VMEM((n_node, cap), jnp.int32),
            pltpu.SMEM((1, n_node), jnp.int32),
            pltpu.VMEM((n_node, cap), f32),
            pltpu.VMEM((tok_rows, features), bf16),
            pltpu.VMEM((units, width), bf16),
            pltpu.VMEM((parts, n_src, cap, piece), bf16),
            pltpu.VMEM((parts, n_src, cap, piece), bf16),
            pltpu.VMEM((parts, n_src, cap, piece), bf16),
            pltpu.VMEM((2, n_ep, own_rows, half), bf16),
            pltpu.VMEM((2 * recv_rows, half), f32),
            pltpu.VMEM((half, 2 * recv_rows), bf16),
            pltpu.VMEM((2 * recv_rows, width), bf16),
            pltpu.VMEM((recv_rows, units), f32),
            pltpu.VMEM((n_ep, own_rows, units), bf16),
            pltpu.VMEM((n_ep, own_rows, units), bf16),
            dma((3,)),
            dma((parts, n_ep)),
            dma((parts,)),
            dma((parts, n_src)),
            dma((parts, n_src)),
            dma((parts, n_src)),
            dma((parts, n_src)),
            dma((2, n_ep)),
            dma((2, n_ep)),
            dma,
            dma((2, parts)),
            dma,
            dma((n_ep,)),
            dma((n_ep,)),
        ],
        compiler_params=pltpu.CompilerParams(
            collective_id=0, has_side_effects=True, vmem_limit_bytes=63 * 2**20
        ),
    )(grad_tokens, slot_token, send_count, route_score, hidden_act, w_down)

    steps = 4
    grad_weight = pl.pallas_call(
        weight_kernel,
        out_shape=jax.ShapeDtypeStruct((1, 1, half, width), bf16),
        in_specs=[hbm, hbm],
        out_specs=hbm,
        scratch_shapes=[
            pltpu.VMEM((half, 2 * recv_rows), bf16),
            pltpu.VMEM((2 * recv_rows, width), bf16),
            pltpu.VMEM((half, width), bf16),
            dma((2,)),
            dma((steps,)),
        ],
        compiler_params=pltpu.CompilerParams(vmem_limit_bytes=63 * 2**20),
    )(hidden, rows)
    return grad_hidden, grad_weight


def solution(mesh):
    sizes = tuple(mesh.shape[name] for name in AXES)
    in_specs = (
        P("pipe", "node", "ep", None, None),
        P("pipe", "node", "ep", None, None),
        P("pipe", "node", "ep", None),
        P("pipe", "node", "ep", None, None),
        P("pipe", "node", "ep", None),
        P("pipe", "node", None, "ep"),
    )
    out_specs = (P("pipe", "node", "ep", None), P("pipe", "node", None, "ep"))
    return jax.shard_map(
        functools.partial(local, sizes),
        mesh=mesh,
        in_specs=in_specs,
        out_specs=out_specs,
        check_vma=False,
    )
```

```python
import functools

import jax
import jax.numpy as jnp
from jax import lax
from jax.experimental import pallas as pl
from jax.experimental.pallas import tpu as pltpu
from jax.sharding import PartitionSpec as P

MESH = pl.DeviceIdType.MESH
AXES = ("pipe", "node", "ep")


def flip(index, mask):
    out = index
    bit = 1
    while bit <= mask:
        if mask & bit:
            out = out + bit * (1 - 2 * ((index // bit) % 2))
        bit *= 2
    return out


def relay_kernel(
    sizes,
    parts,
    tokens,
    slots,
    counts,
    scores,
    hidden,
    weight,
    rows_out,
    hidden_out,
    shares_out,
    slots_v,
    counts_v,
    scores_v,
    tok_v,
    weight_v,
    send,
    recv,
    mirrored,
    hid,
    hid_all,
    hid_turned,
    rows_all,
    total,
    part_send,
    part_recv,
    small_sem,
    tok_sem,
    weight_sem,
    send_sem,
    recv_sem,
    fwd_sem,
    mir_sem,
    hsend_sem,
    hrecv_sem,
    hloc_sem,
    rows_sem,
    turned_sem,
    shares_sem,
    psend_sem,
    precv_sem,
):
    n_pipe, n_node, n_ep = sizes
    n_src = n_node * n_ep
    cap, piece = send.shape[2], send.shape[3]
    width = piece * parts
    tok_rows = tok_v.shape[0]
    own_rows = hid.shape[2]
    half = hid.shape[3]
    recv_rows = n_src * cap

    pipe, node, ep = (lax.axis_index(name) for name in AXES)
    mirror = n_pipe - 1 - pipe
    me = node * n_ep + ep
    keep_first = (pipe // (n_pipe // 2)) * half
    give_first = half - keep_first

    small_loads = [
        pltpu.make_async_copy(slots.at[0, 0, 0], slots_v, small_sem.at[0]),
        pltpu.make_async_copy(counts.at[0, 0], counts_v, small_sem.at[1]),
        pltpu.make_async_copy(scores.at[0, 0, 0], scores_v, small_sem.at[2]),
    ]
    for load in small_loads:
        load.start()
    tok_loads = {}
    for c in range(parts):
        for e in range(n_ep):
            cols = pl.ds(e * width + c * piece, piece)
            tok_loads[c, e] = pltpu.make_async_copy(
                tokens.at[0, 0, 0, :, cols], tok_v.at[:, cols], tok_sem.at[c, e]
            )
            tok_loads[c, e].start()
    hid_load = pltpu.make_async_copy(
        hidden.at[0, 0, :, pl.ds(pl.multiple_of(keep_first, 128), half)],
        hid.at[0, ep],
        hloc_sem,
    )
    hid_load.start()
    weight_loads = []
    for c in range(parts):
        cols = pl.ds(c * piece, piece)
        load = pltpu.make_async_copy(
            weight.at[0, 0, :, cols], weight_v.at[:, cols], weight_sem.at[c]
        )
        load.start()
        weight_loads.append(load)

    barrier = pltpu.get_barrier_semaphore()
    peers = [
        (pipe, flip(node, k), flip(ep, j))
        for k in range(n_node)
        for j in range(n_ep)
        if k or j
    ] + [(mirror, node, flip(ep, j)) for j in range(n_ep)]
    for peer in peers:
        pl.semaphore_signal(barrier, inc=1, device_id=peer, device_id_type=MESH)

    eye = lax.broadcasted_iota(jnp.int32, (cap, cap), 0) == lax.broadcasted_iota(
        jnp.int32, (cap, cap), 1
    )
    slot_ids = lax.broadcasted_iota(jnp.int32, (cap, 1), 0)
    token_ids = lax.broadcasted_iota(jnp.int32, (cap, tok_rows), 1)
    hot, factor = [], []
    for load in small_loads:
        load.wait()
    for g in range(n_node):
        slot_row = slots_v[g : g + 1, :]
        score_row = scores_v[g : g + 1, :]
        slot_col = jnp.sum(jnp.where(eye, slot_row, 0), axis=1, keepdims=True)
        score_col = jnp.sum(jnp.where(eye, score_row, 0.0), axis=1, keepdims=True)
        hot.append(jnp.where(token_ids == slot_col, 1.0, 0.0))
        factor.append(jnp.where(slot_ids < counts_v[0, g], score_col, 0.0))
    hot = jnp.concatenate(hot, axis=0).astype(jnp.bfloat16)
    factor = jnp.concatenate(factor, axis=0)

    def route(c):
        for e in range(n_ep):
            tok_loads[c, e].wait()
            start = e * width + c * piece
            picked = jnp.dot(
                hot, tok_v[:, start : start + piece], preferred_element_type=jnp.float32
            )
            picked = picked * factor
            for g in range(n_node):
                send[c, g * n_ep + e] = picked[g * cap : (g + 1) * cap].astype(jnp.bfloat16)

    sent, stores = [], []

    def store_rows(c, at, value):
        block = (pl.ds(at * recv_rows, recv_rows), pl.ds(c * piece, piece))
        rows_all[block] = value
        store = pltpu.make_async_copy(
            rows_all.at[block], rows_out.at[block], rows_sem.at[at, c]
        )
        store.start()
        stores.append(store)

    def dispatch(c):
        for k in range(n_node):
            for j in range(n_ep):
                if k == 0 and j == 0:
                    continue
                to_node, to_ep = flip(node, k), flip(ep, j)
                copy = pltpu.make_async_remote_copy(
                    src_ref=send.at[c, to_node * n_ep + to_ep],
                    dst_ref=recv.at[c, me],
                    send_sem=send_sem.at[c, k * n_ep + j],
                    recv_sem=recv_sem.at[c, me],
                    device_id=(pipe, to_node, to_ep),
                    device_id_type=MESH,
                )
                copy.start()
                sent.append(copy)

    def forward(c, source, index, block):
        copy = pltpu.make_async_remote_copy(
            src_ref=block,
            dst_ref=mirrored.at[c, source],
            send_sem=fwd_sem.at[c, index],
            recv_sem=mir_sem.at[c, source],
            device_id=(mirror, node, ep),
            device_id_type=MESH,
        )
        copy.start()
        sent.append(copy)

    route(0)
    pl.semaphore_wait(barrier, len(peers))
    dispatch(0)
    forward(0, me, 0, send.at[0, me])
    for j in range(n_ep):
        copy = pltpu.make_async_remote_copy(
            src_ref=hidden.at[0, 0, :, pl.ds(pl.multiple_of(give_first, 128), half)],
            dst_ref=hid.at[1, ep],
            send_sem=hsend_sem.at[1, j],
            recv_sem=hrecv_sem.at[1, ep],
            device_id=(mirror, node, flip(ep, j)),
            device_id_type=MESH,
        )
        copy.start()
        sent.append(copy)
        if j:
            copy = pltpu.make_async_remote_copy(
                src_ref=hidden.at[0, 0, :, pl.ds(pl.multiple_of(keep_first, 128), half)],
                dst_ref=hid.at[0, ep],
                send_sem=hsend_sem.at[0, j],
                recv_sem=hrecv_sem.at[0, ep],
                device_id=(pipe, node, flip(ep, j)),
                device_id_type=MESH,
            )
            copy.start()
            sent.append(copy)
    for c in range(1, parts):
        route(c)
        dispatch(c)
        forward(c, me, 0, send.at[c, me])
    for c in range(parts):
        recv[c, me] = send[c, me]

    def arrival(buffer, index, sem):
        return pltpu.make_async_remote_copy(
            src_ref=buffer.at[index],
            dst_ref=buffer.at[index],
            send_sem=send_sem.at[0, 0],
            recv_sem=sem.at[index],
            device_id=(mirror, node, ep),
            device_id_type=MESH,
        )

    def gathered(buffer, c):
        blocks = [buffer[c, s].astype(jnp.float32) for s in range(n_src)]
        return jnp.concatenate(blocks, axis=0).astype(jnp.bfloat16)

    hid_load.wait()
    for j in range(n_ep):
        source = flip(ep, j)
        arrival(hid, (1, source), hrecv_sem).wait_recv()
        if j:
            arrival(hid, (0, source), hrecv_sem).wait_recv()
    for copy_at in range(2):
        for e in range(n_ep):
            first = (copy_at * n_ep + e) * own_rows
            hid_all[first : first + own_rows, :] = hid[copy_at, e].astype(jnp.float32)
    hid_turned[...] = hid_all[...].T.astype(jnp.bfloat16)
    store = pltpu.make_async_copy(hid_turned, hidden_out, turned_sem)
    store.start()
    stores.append(store)

    for c in range(parts):
        for k in range(n_node):
            for j in range(n_ep):
                if k == 0 and j == 0:
                    continue
                source = flip(node, k) * n_ep + flip(ep, j)
                arrival(recv, (c, source), recv_sem).wait_recv()
                forward(c, source, k * n_ep + j, recv.at[c, source])
        rows = gathered(recv, c)
        store_rows(c, 0, rows)
        weight_loads[c].wait()
        share = lax.dot_general(
            rows,
            weight_v[:, c * piece : (c + 1) * piece],
            (((1,), (1,)), ((), ())),
            preferred_element_type=jnp.float32,
        )
        if c == 0:
            total[...] = share
        else:
            total[...] += share

    first = pl.multiple_of(ep * own_rows, own_rows)
    part_send[0] = total[pl.ds(first, own_rows), :].astype(jnp.bfloat16)
    store = pltpu.make_async_copy(part_send.at[0], shares_out.at[ep], shares_sem.at[0])
    store.start()
    stores.append(store)
    for j in range(1, n_ep):
        to_ep = flip(ep, j)
        first = pl.multiple_of(to_ep * own_rows, own_rows)
        part_send[j] = total[pl.ds(first, own_rows), :].astype(jnp.bfloat16)
        copy = pltpu.make_async_remote_copy(
            src_ref=part_send.at[j],
            dst_ref=part_recv.at[ep],
            send_sem=psend_sem.at[j],
            recv_sem=precv_sem.at[ep],
            device_id=(pipe, node, to_ep),
            device_id_type=MESH,
        )
        copy.start()
        sent.append(copy)

    for c in range(parts):
        for k in range(n_node):
            for j in range(n_ep):
                source = flip(node, k) * n_ep + flip(ep, j)
                arrival(mirrored, (c, source), mir_sem).wait_recv()
        store_rows(c, 1, gathered(mirrored, c))

    for j in range(1, n_ep):
        source = flip(ep, j)
        arrival(part_recv, (source,), precv_sem).wait_recv()
        store = pltpu.make_async_copy(
            part_recv.at[source], shares_out.at[source], shares_sem.at[j]
        )
        store.start()
        stores.append(store)
    for copy in sent:
        copy.wait_send()
    for store in stores:
        store.wait()


def weight_kernel(
    hidden,
    rows,
    shares,
    grad_hidden,
    grad_weight,
    hid_v,
    rows_v,
    shares_v,
    small_v,
    out_v,
    load_sem,
    small_sem,
    store_sem,
):
    loads = [
        pltpu.make_async_copy(hidden, hid_v, load_sem.at[0]),
        pltpu.make_async_copy(rows, rows_v, load_sem.at[1]),
        pltpu.make_async_copy(shares, shares_v, load_sem.at[2]),
    ]
    for load in loads:
        load.start()
    for load in loads[:2]:
        load.wait()
    steps = store_sem.shape[0]
    tall = hid_v.shape[0] // steps
    stores = []
    for m in range(steps):
        block = pl.ds(m * tall, tall)
        out_v[block, :] = jnp.dot(
            hid_v[block, :], rows_v[...], preferred_element_type=jnp.float32
        ).astype(jnp.bfloat16)
        store = pltpu.make_async_copy(
            out_v.at[block, :], grad_weight.at[0, 0, block, :], store_sem.at[m]
        )
        store.start()
        stores.append(store)
        if m == 0:
            loads[2].wait()
            summed = shares_v[0].astype(jnp.float32)
            for e in range(1, shares_v.shape[0]):
                summed = summed + shares_v[e].astype(jnp.float32)
            small_v[...] = summed.astype(jnp.bfloat16)
            store = pltpu.make_async_copy(small_v, grad_hidden.at[0, 0], small_sem)
            store.start()
            stores.append(store)
    for store in stores:
        store.wait()


def local(sizes, grad_tokens, slot_token, send_count, route_score, hidden_act, w_down):
    n_pipe, n_node, n_ep = sizes
    n_src = n_node * n_ep
    tok_rows, features = grad_tokens.shape[-2:]
    cap = slot_token.shape[-1]
    own_rows, units = hidden_act.shape[-2:]
    width = w_down.shape[-1]
    half = units // 2
    recv_rows = n_src * cap
    parts = 2 if (width // 128) % 2 == 0 else 1
    piece = width // parts
    bf16, f32 = jnp.bfloat16, jnp.float32
    dma = pltpu.SemaphoreType.DMA
    hbm = pl.BlockSpec(memory_space=pltpu.HBM)
    rows, hidden, shares = pl.pallas_call(
        functools.partial(relay_kernel, sizes, parts),
        out_shape=(
            jax.ShapeDtypeStruct((2 * recv_rows, width), bf16),
            jax.ShapeDtypeStruct((half, 2 * recv_rows), bf16),
            jax.ShapeDtypeStruct((n_ep, own_rows, units), bf16),
        ),
        in_specs=[hbm] * 6,
        out_specs=(hbm, hbm, hbm),
        scratch_shapes=[
            pltpu.VMEM((n_node, cap), jnp.int32),
            pltpu.SMEM((1, n_node), jnp.int32),
            pltpu.VMEM((n_node, cap), f32),
            pltpu.VMEM((tok_rows, features), bf16),
            pltpu.VMEM((units, width), bf16),
            pltpu.VMEM((parts, n_src, cap, piece), bf16),
            pltpu.VMEM((parts, n_src, cap, piece), bf16),
            pltpu.VMEM((parts, n_src, cap, piece), bf16),
            pltpu.VMEM((2, n_ep, own_rows, half), bf16),
            pltpu.VMEM((2 * recv_rows, half), f32),
            pltpu.VMEM((half, 2 * recv_rows), bf16),
            pltpu.VMEM((2 * recv_rows, width), bf16),
            pltpu.VMEM((recv_rows, units), f32),
            pltpu.VMEM((n_ep, own_rows, units), bf16),
            pltpu.VMEM((n_ep, own_rows, units), bf16),
            dma((3,)),
            dma((parts, n_ep)),
            dma((parts,)),
            dma((parts, n_src)),
            dma((parts, n_src)),
            dma((parts, n_src)),
            dma((parts, n_src)),
            dma((2, n_ep)),
            dma((2, n_ep)),
            dma,
            dma((2, parts)),
            dma,
            dma((n_ep,)),
            dma((n_ep,)),
            dma((n_ep,)),
        ],
        compiler_params=pltpu.CompilerParams(
            collective_id=0, has_side_effects=True, vmem_limit_bytes=63 * 2**20
        ),
    )(grad_tokens, slot_token, send_count, route_score, hidden_act, w_down)

    steps = 8
    return pl.pallas_call(
        weight_kernel,
        out_shape=(
            jax.ShapeDtypeStruct((1, 1, own_rows, units), bf16),
            jax.ShapeDtypeStruct((1, 1, half, width), bf16),
        ),
        in_specs=[hbm, hbm, hbm],
        out_specs=(hbm, hbm),
        scratch_shapes=[
            pltpu.VMEM((half, 2 * recv_rows), bf16),
            pltpu.VMEM((2 * recv_rows, width), bf16),
            pltpu.VMEM((n_ep, own_rows, units), bf16),
            pltpu.VMEM((own_rows, units), bf16),
            pltpu.VMEM((half, width), bf16),
            dma((3,)),
            dma,
            dma((steps,)),
        ],
        compiler_params=pltpu.CompilerParams(vmem_limit_bytes=63 * 2**20),
    )(hidden, rows, shares)


def solution(mesh):
    sizes = tuple(mesh.shape[name] for name in AXES)
    in_specs = (
        P("pipe", "node", "ep", None, None),
        P("pipe", "node", "ep", None, None),
        P("pipe", "node", "ep", None),
        P("pipe", "node", "ep", None, None),
        P("pipe", "node", "ep", None),
        P("pipe", "node", None, "ep"),
    )
    out_specs = (P("pipe", "node", "ep", None), P("pipe", "node", None, "ep"))
    return jax.shard_map(
        functools.partial(local, sizes),
        mesh=mesh,
        in_specs=in_specs,
        out_specs=out_specs,
        check_vma=False,
    )
```

```python
import functools

import jax
import jax.numpy as jnp
from jax import lax
from jax.experimental import pallas as pl
from jax.experimental.pallas import tpu as pltpu
from jax.sharding import PartitionSpec as P

MESH = pl.DeviceIdType.MESH
AXES = ("pipe", "node", "ep")


def flip(index, mask):
    out = index
    bit = 1
    while bit <= mask:
        if mask & bit:
            out = out + bit * (1 - 2 * ((index // bit) % 2))
        bit *= 2
    return out


def relay_kernel(
    sizes,
    parts,
    tokens,
    slots,
    counts,
    scores,
    hidden,
    weight,
    rows_out,
    hidden_out,
    shares_out,
    slots_v,
    counts_v,
    scores_v,
    tok_v,
    weight_v,
    send,
    recv,
    mirrored,
    hid,
    hid_all,
    hid_turned,
    rows_all,
    total,
    part_send,
    part_recv,
    small_sem,
    tok_sem,
    weight_sem,
    send_sem,
    recv_sem,
    fwd_sem,
    mir_sem,
    hsend_sem,
    hrecv_sem,
    hloc_sem,
    rows_sem,
    turned_sem,
    shares_sem,
    psend_sem,
    precv_sem,
):
    n_pipe, n_node, n_ep = sizes
    n_src = n_node * n_ep
    cap, piece = send.shape[2], send.shape[3]
    width = piece * parts
    tok_rows = tok_v.shape[0]
    own_rows = hid.shape[2]
    half = hid.shape[3]
    recv_rows = n_src * cap

    pipe, node, ep = (lax.axis_index(name) for name in AXES)
    mirror = n_pipe - 1 - pipe
    me = node * n_ep + ep
    keep_first = (pipe // (n_pipe // 2)) * half
    give_first = half - keep_first

    small_loads = [
        pltpu.make_async_copy(slots.at[0, 0, 0], slots_v, small_sem.at[0]),
        pltpu.make_async_copy(counts.at[0, 0], counts_v, small_sem.at[1]),
        pltpu.make_async_copy(scores.at[0, 0, 0], scores_v, small_sem.at[2]),
    ]
    for load in small_loads:
        load.start()
    tok_loads = {}
    for c in range(parts):
        for e in range(n_ep):
            cols = pl.ds(e * width + c * piece, piece)
            tok_loads[c, e] = pltpu.make_async_copy(
                tokens.at[0, 0, 0, :, cols], tok_v.at[:, cols], tok_sem.at[c, e]
            )
            tok_loads[c, e].start()
    hid_load = pltpu.make_async_copy(
        hidden.at[0, 0, :, pl.ds(pl.multiple_of(keep_first, 128), half)],
        hid.at[0, ep],
        hloc_sem,
    )
    hid_load.start()
    weight_loads = []
    for c in range(parts):
        cols = pl.ds(c * piece, piece)
        load = pltpu.make_async_copy(
            weight.at[0, 0, :, cols], weight_v.at[:, cols], weight_sem.at[c]
        )
        load.start()
        weight_loads.append(load)

    barrier = pltpu.get_barrier_semaphore()
    peers = [
        (pipe, flip(node, k), flip(ep, j))
        for k in range(n_node)
        for j in range(n_ep)
        if k or j
    ] + [(mirror, node, flip(ep, j)) for j in range(n_ep)]
    for peer in peers:
        pl.semaphore_signal(barrier, inc=1, device_id=peer, device_id_type=MESH)

    eye = lax.broadcasted_iota(jnp.int32, (cap, cap), 0) == lax.broadcasted_iota(
        jnp.int32, (cap, cap), 1
    )
    slot_ids = lax.broadcasted_iota(jnp.int32, (cap, 1), 0)
    token_ids = lax.broadcasted_iota(jnp.int32, (cap, tok_rows), 1)
    hot, factor = [], []
    for load in small_loads:
        load.wait()
    for g in range(n_node):
        slot_row = slots_v[g : g + 1, :]
        score_row = scores_v[g : g + 1, :]
        slot_col = jnp.sum(jnp.where(eye, slot_row, 0), axis=1, keepdims=True)
        score_col = jnp.sum(jnp.where(eye, score_row, 0.0), axis=1, keepdims=True)
        hot.append(jnp.where(token_ids == slot_col, 1.0, 0.0))
        factor.append(jnp.where(slot_ids < counts_v[0, g], score_col, 0.0))
    hot = jnp.concatenate(hot, axis=0).astype(jnp.bfloat16)
    factor = jnp.concatenate(factor, axis=0)

    def route(c):
        for e in range(n_ep):
            tok_loads[c, e].wait()
            start = e * width + c * piece
            picked = jnp.dot(
                hot, tok_v[:, start : start + piece], preferred_element_type=jnp.float32
            )
            picked = picked * factor
            for g in range(n_node):
                send[c, g * n_ep + e] = picked[g * cap : (g + 1) * cap].astype(jnp.bfloat16)

    sent, stores = [], []

    def store_rows(c, at, value):
        block = (pl.ds(at * recv_rows, recv_rows), pl.ds(c * piece, piece))
        rows_all[block] = value
        store = pltpu.make_async_copy(
            rows_all.at[block], rows_out.at[block], rows_sem.at[at, c]
        )
        store.start()
        stores.append(store)

    def dispatch(c):
        for k in range(n_node):
            for j in range(n_ep):
                if k == 0 and j == 0:
                    continue
                to_node, to_ep = flip(node, k), flip(ep, j)
                copy = pltpu.make_async_remote_copy(
                    src_ref=send.at[c, to_node * n_ep + to_ep],
                    dst_ref=recv.at[c, me],
                    send_sem=send_sem.at[c, k * n_ep + j],
                    recv_sem=recv_sem.at[c, me],
                    device_id=(pipe, to_node, to_ep),
                    device_id_type=MESH,
                )
                copy.start()
                sent.append(copy)

    def forward(c, source, index, block):
        copy = pltpu.make_async_remote_copy(
            src_ref=block,
            dst_ref=mirrored.at[c, source],
            send_sem=fwd_sem.at[c, index],
            recv_sem=mir_sem.at[c, source],
            device_id=(mirror, node, ep),
            device_id_type=MESH,
        )
        copy.start()
        sent.append(copy)

    route(0)
    pl.semaphore_wait(barrier, len(peers))
    dispatch(0)
    forward(0, me, 0, send.at[0, me])
    for j in range(n_ep):
        copy = pltpu.make_async_remote_copy(
            src_ref=hidden.at[0, 0, :, pl.ds(pl.multiple_of(give_first, 128), half)],
            dst_ref=hid.at[1, ep],
            send_sem=hsend_sem.at[1, j],
            recv_sem=hrecv_sem.at[1, ep],
            device_id=(mirror, node, flip(ep, j)),
            device_id_type=MESH,
        )
        copy.start()
        sent.append(copy)
        if j:
            copy = pltpu.make_async_remote_copy(
                src_ref=hidden.at[0, 0, :, pl.ds(pl.multiple_of(keep_first, 128), half)],
                dst_ref=hid.at[0, ep],
                send_sem=hsend_sem.at[0, j],
                recv_sem=hrecv_sem.at[0, ep],
                device_id=(pipe, node, flip(ep, j)),
                device_id_type=MESH,
            )
            copy.start()
            sent.append(copy)
    for c in range(1, parts):
        route(c)
        dispatch(c)
        forward(c, me, 0, send.at[c, me])
    for c in range(parts):
        recv[c, me] = send[c, me]

    def arrival(buffer, index, sem):
        return pltpu.make_async_remote_copy(
            src_ref=buffer.at[index],
            dst_ref=buffer.at[index],
            send_sem=send_sem.at[0, 0],
            recv_sem=sem.at[index],
            device_id=(mirror, node, ep),
            device_id_type=MESH,
        )

    def gathered(buffer, c):
        blocks = [buffer[c, s].astype(jnp.float32) for s in range(n_src)]
        return jnp.concatenate(blocks, axis=0).astype(jnp.bfloat16)

    hid_load.wait()
    for j in range(n_ep):
        source = flip(ep, j)
        arrival(hid, (1, source), hrecv_sem).wait_recv()
        if j:
            arrival(hid, (0, source), hrecv_sem).wait_recv()
    for copy_at in range(2):
        for e in range(n_ep):
            first = (copy_at * n_ep + e) * own_rows
            hid_all[first : first + own_rows, :] = hid[copy_at, e].astype(jnp.float32)
    hid_turned[...] = hid_all[...].T.astype(jnp.bfloat16)
    store = pltpu.make_async_copy(hid_turned, hidden_out, turned_sem)
    store.start()
    stores.append(store)

    for c in range(parts):
        for k in range(n_node):
            for j in range(n_ep):
                if k == 0 and j == 0:
                    continue
                source = flip(node, k) * n_ep + flip(ep, j)
                arrival(recv, (c, source), recv_sem).wait_recv()
                forward(c, source, k * n_ep + j, recv.at[c, source])
        rows = gathered(recv, c)
        store_rows(c, 0, rows)
        weight_loads[c].wait()
        share = lax.dot_general(
            rows,
            weight_v[:, c * piece : (c + 1) * piece],
            (((1,), (1,)), ((), ())),
            preferred_element_type=jnp.float32,
        )
        if c == 0:
            total[...] = share
        else:
            total[...] += share

    first = pl.multiple_of(ep * own_rows, own_rows)
    part_send[0] = total[pl.ds(first, own_rows), :].astype(jnp.bfloat16)
    store = pltpu.make_async_copy(part_send.at[0], shares_out.at[ep], shares_sem.at[0])
    store.start()
    stores.append(store)
    for j in range(1, n_ep):
        to_ep = flip(ep, j)
        first = pl.multiple_of(to_ep * own_rows, own_rows)
        part_send[j] = total[pl.ds(first, own_rows), :].astype(jnp.bfloat16)
        copy = pltpu.make_async_remote_copy(
            src_ref=part_send.at[j],
            dst_ref=part_recv.at[ep],
            send_sem=psend_sem.at[j],
            recv_sem=precv_sem.at[ep],
            device_id=(pipe, node, to_ep),
            device_id_type=MESH,
        )
        copy.start()
        sent.append(copy)

    for c in range(parts):
        for k in range(n_node):
            for j in range(n_ep):
                source = flip(node, k) * n_ep + flip(ep, j)
                arrival(mirrored, (c, source), mir_sem).wait_recv()
        store_rows(c, 1, gathered(mirrored, c))

    for j in range(1, n_ep):
        source = flip(ep, j)
        arrival(part_recv, (source,), precv_sem).wait_recv()
        store = pltpu.make_async_copy(
            part_recv.at[source], shares_out.at[source], shares_sem.at[j]
        )
        store.start()
        stores.append(store)
    for copy in sent:
        copy.wait_send()
    for store in stores:
        store.wait()


def weight_kernel(
    hidden,
    rows,
    shares,
    grad_hidden,
    grad_weight,
    hid_v,
    rows_v,
    shares_v,
    small_v,
    out_v,
    load_sem,
    small_sem,
    store_sem,
):
    loads = [
        pltpu.make_async_copy(hidden, hid_v, load_sem.at[0]),
        pltpu.make_async_copy(shares, shares_v, load_sem.at[1]),
    ]
    pieces, steps = store_sem.shape
    span = rows_v.shape[1] // pieces
    for n in range(pieces):
        cols = pl.ds(n * span, span)
        loads.append(
            pltpu.make_async_copy(rows.at[:, cols], rows_v.at[:, cols], load_sem.at[2 + n])
        )
    for load in loads:
        load.start()
    loads[0].wait()
    tall = hid_v.shape[0] // steps
    stores = []
    for n in range(pieces):
        loads[2 + n].wait()
        cols = pl.ds(n * span, span)
        for m in range(steps):
            block = pl.ds(m * tall, tall)
            out_v[block, cols] = jnp.dot(
                hid_v[block, :], rows_v[:, cols], preferred_element_type=jnp.float32
            ).astype(jnp.bfloat16)
            store = pltpu.make_async_copy(
                out_v.at[block, cols], grad_weight.at[0, 0, block, cols], store_sem.at[n, m]
            )
            store.start()
            stores.append(store)
            if n == 0 and m == 0:
                loads[1].wait()
                summed = shares_v[0].astype(jnp.float32)
                for e in range(1, shares_v.shape[0]):
                    summed = summed + shares_v[e].astype(jnp.float32)
                small_v[...] = summed.astype(jnp.bfloat16)
                store = pltpu.make_async_copy(small_v, grad_hidden.at[0, 0], small_sem)
                store.start()
                stores.append(store)
    for store in stores:
        store.wait()


def local(sizes, grad_tokens, slot_token, send_count, route_score, hidden_act, w_down):
    n_pipe, n_node, n_ep = sizes
    n_src = n_node * n_ep
    tok_rows, features = grad_tokens.shape[-2:]
    cap = slot_token.shape[-1]
    own_rows, units = hidden_act.shape[-2:]
    width = w_down.shape[-1]
    half = units // 2
    recv_rows = n_src * cap
    parts = 2 if (width // 128) % 2 == 0 else 1
    piece = width // parts
    bf16, f32 = jnp.bfloat16, jnp.float32
    dma = pltpu.SemaphoreType.DMA
    hbm = pl.BlockSpec(memory_space=pltpu.HBM)
    rows, hidden, shares = pl.pallas_call(
        functools.partial(relay_kernel, sizes, parts),
        out_shape=(
            jax.ShapeDtypeStruct((2 * recv_rows, width), bf16),
            jax.ShapeDtypeStruct((half, 2 * recv_rows), bf16),
            jax.ShapeDtypeStruct((n_ep, own_rows, units), bf16),
        ),
        in_specs=[hbm] * 6,
        out_specs=(hbm, hbm, hbm),
        scratch_shapes=[
            pltpu.VMEM((n_node, cap), jnp.int32),
            pltpu.SMEM((1, n_node), jnp.int32),
            pltpu.VMEM((n_node, cap), f32),
            pltpu.VMEM((tok_rows, features), bf16),
            pltpu.VMEM((units, width), bf16),
            pltpu.VMEM((parts, n_src, cap, piece), bf16),
            pltpu.VMEM((parts, n_src, cap, piece), bf16),
            pltpu.VMEM((parts, n_src, cap, piece), bf16),
            pltpu.VMEM((2, n_ep, own_rows, half), bf16),
            pltpu.VMEM((2 * recv_rows, half), f32),
            pltpu.VMEM((half, 2 * recv_rows), bf16),
            pltpu.VMEM((2 * recv_rows, width), bf16),
            pltpu.VMEM((recv_rows, units), f32),
            pltpu.VMEM((n_ep, own_rows, units), bf16),
            pltpu.VMEM((n_ep, own_rows, units), bf16),
            dma((3,)),
            dma((parts, n_ep)),
            dma((parts,)),
            dma((parts, n_src)),
            dma((parts, n_src)),
            dma((parts, n_src)),
            dma((parts, n_src)),
            dma((2, n_ep)),
            dma((2, n_ep)),
            dma,
            dma((2, parts)),
            dma,
            dma((n_ep,)),
            dma((n_ep,)),
            dma((n_ep,)),
        ],
        compiler_params=pltpu.CompilerParams(
            collective_id=0, has_side_effects=True, vmem_limit_bytes=63 * 2**20
        ),
    )(grad_tokens, slot_token, send_count, route_score, hidden_act, w_down)

    steps = 4
    return pl.pallas_call(
        weight_kernel,
        out_shape=(
            jax.ShapeDtypeStruct((1, 1, own_rows, units), bf16),
            jax.ShapeDtypeStruct((1, 1, half, width), bf16),
        ),
        in_specs=[hbm, hbm, hbm],
        out_specs=(hbm, hbm),
        scratch_shapes=[
            pltpu.VMEM((half, 2 * recv_rows), bf16),
            pltpu.VMEM((2 * recv_rows, width), bf16),
            pltpu.VMEM((n_ep, own_rows, units), bf16),
            pltpu.VMEM((own_rows, units), bf16),
            pltpu.VMEM((half, width), bf16),
            dma((2 + parts,)),
            dma,
            dma((parts, steps)),
        ],
        compiler_params=pltpu.CompilerParams(vmem_limit_bytes=63 * 2**20),
    )(hidden, rows, shares)


def solution(mesh):
    sizes = tuple(mesh.shape[name] for name in AXES)
    in_specs = (
        P("pipe", "node", "ep", None, None),
        P("pipe", "node", "ep", None, None),
        P("pipe", "node", "ep", None),
        P("pipe", "node", "ep", None, None),
        P("pipe", "node", "ep", None),
        P("pipe", "node", None, "ep"),
    )
    out_specs = (P("pipe", "node", "ep", None), P("pipe", "node", None, "ep"))
    return jax.shard_map(
        functools.partial(local, sizes),
        mesh=mesh,
        in_specs=in_specs,
        out_specs=out_specs,
        check_vma=False,
    )
```
